256 devices in a mesh: section: 8 (over x_lo, y), rep: 32 (over z, x_hi, core).
Axes of the slice: x: 4 (x_hi: 2, x_lo: 2; x = x_hi * 2 + x_lo), y: 4, z: 8, core: 2. Of those that a mesh axis runs over, the one named last changes fastest.
Arguments:
- inputs: bfloat16 [6, 1024, 6144], P(None, 'rep'), may hold values from -6 to 6
- cotangent: bfloat16 [6, 1024, 6144], P(None, 'rep'), may hold values from -6 to 6
- in_weight: bfloat16 [8, 6144, 256], P('section', 'rep'), may hold values from -0.078125 to 0.078125
- out_weight: bfloat16 [8, 6144, 256], P('section', 'rep'), may hold values from -0.375 to 0.375
- norm_gain: float32 [8, 6144], P('section'), may hold values from 0.5 to 1.5
- lengths: int32 [32, 6], P('rep'), may hold values from 1 to 32, 144 in all within a row
Outputs:
- grad_in_weight: bfloat16 [8, 6144, 256], P('section', 'rep')
- grad_out_weight: bfloat16 [8, 6144, 256], P('section', 'rep')
- grad_gain: float32 [8, 6144], P('section')
- grad_inputs: bfloat16 [8, 6, 1024, 6144], P('section', None, 'rep')
The draws below stay inside these ranges and needn't reach their ends.
Inputs may be any that keep to these rules, and one draw needn't show every extreme that they name: `lengths`: each replica's 6 counts sum to 144 and the largest is 32.
All inputs are finite; a program needn't handle non-finite values.
Results may differ from the reference program's by a relative error of at most 0.025.
Values may be sent and summed in bfloat16 or wider, within the bound.
No kernel may reach another device: no remote copies, remote signals or barrier semaphores. Data moves between devices by JAX's collectives and lax.ppermute only.
A program may use at most 64 MiB of HBM per device.

```python
import math
import jax
import jax.numpy as jnp
import numpy as np
from jax import lax

D = 6144
LATENT = 256
MICRO = 6
TOK_MB = 32
BATCH_ROWS = 1024
ALL_ROWS = 6144
N_SECTION = 8
N_REP = 32


def block_levels(key, dims, pieces, smallest, largest):
    gain = 1.0
    for dim, parts in pieces:
        draws = jax.random.uniform(jax.random.fold_in(jax.random.fold_in(key, 6), dim), (parts,), jnp.float32, smallest / len(pieces), largest / len(pieces))
        gain = gain * jnp.repeat(jnp.exp(draws), dims[dim] // parts).reshape((-1,) + (1,) * (len(dims) - 1 - dim))
    return gain


def length_profile(amount, total, reach, skew):
    loads = [(1 << 20) // math.isqrt(grade ** skew) + 1 for grade in range(2, amount + 1)]
    rest, counts = total - reach - (amount - 1), [1] * (amount - 1)
    while rest > 0:
        free = [i for i in range(amount - 1) if counts[i] < reach]
        whole, remaining = sum([loads[i] for i in free]), rest
        for i in free:
            addition = min(reach - counts[i], max(1, remaining * loads[i] // whole), rest)
            counts[i] = counts[i] + addition
            rest = rest - addition
    return np.array([reach] + counts)


def uneven_parts(key, count, total, most, lean):
    if count == 2:
        one = jax.random.randint(key, (), max(1, total - most), min(most, total - 1) + 1)
        return jnp.stack([one, total - one])
    sizes = jnp.asarray(length_profile(count, total, most, lean), jnp.int32)
    pairs = (count - 1) // 2
    giver, receiver = sizes[1:1 + 2 * pairs:2], sizes[2:2 + 2 * pairs:2]
    slack = jnp.minimum(giver - 1, most - receiver)
    passed = jax.random.randint(jax.random.fold_in(key, 1), (pairs,), 0, 1 << 20) % (slack + 1)
    sizes = sizes.at[1:1 + 2 * pairs:2].set(giver - passed).at[2:2 + 2 * pairs:2].set(receiver + passed)
    return sizes[jax.random.permutation(jax.random.fold_in(key, 2), count)]


def normal_values(stream_key, dims, deviation, limit, shards=(), kind=jnp.bfloat16):
    result = jax.random.normal(stream_key, dims, jnp.float32) * deviation
    if len(shards) > 0:
        result = block_levels(stream_key, dims, shards, -0.22, 0.18) * result
    return jnp.clip(result, min=-limit, max=limit).astype(kind)


def setup_inputs(seed: int = 0) -> dict:
    splits = jax.random.split(jax.random.key(seed), 7)
    return {
        "inputs": normal_values(splits[0], (MICRO, BATCH_ROWS, D), 1.0, 6.0, ((1, 32),)),
        "cotangent": normal_values(splits[1], (MICRO, BATCH_ROWS, D), 1.0, 6.0, ((1, 32),)),
        "in_weight": normal_values(splits[2], (N_SECTION, D, LATENT), D ** -0.5, 0.078125, ((0, 8), (1, 32))),
        "out_weight": normal_values(splits[3], (N_SECTION, D, LATENT), LATENT ** -0.5, 0.375, ((0, 8), (1, 32))),
        "norm_gain": jnp.clip(1.0 + 0.1 * jax.random.normal(splits[4], (N_SECTION, D), jnp.float32), 0.5, 1.5),
        "lengths": jax.vmap(lambda own: uneven_parts(own, MICRO, MICRO * TOK_MB * 3 // 4, TOK_MB, 2))(jax.random.split(splits[5], N_REP)).reshape((N_REP, MICRO)).astype(jnp.int32),
    }


norm_epsilon = 1e-05

def section_forward(hidden, norm_gain, in_weight, out_weight):
    widened = hidden.astype(jnp.float32)
    inverse = lax.rsqrt(lax.optimization_barrier(jnp.mean(widened * widened, axis=-1, keepdims=True)) + norm_epsilon)
    normed = (widened * inverse * norm_gain).astype(jnp.bfloat16)
    before = jnp.dot(normed, in_weight, preferred_element_type=jnp.float32)
    activated = jax.nn.silu(before).astype(jnp.bfloat16)
    mixed = lax.dot_general(activated, out_weight, (((1,), (1,)), ((), ())), preferred_element_type=jnp.float32)
    return ((widened + mixed).astype(jnp.bfloat16), normed, before, activated)

def section_backward(hidden, norm_gain, in_weight, out_weight, before, upstream):
    widened = hidden.astype(jnp.float32)
    inverse = lax.rsqrt(lax.optimization_barrier(jnp.mean(widened * widened, axis=-1, keepdims=True)) + norm_epsilon)
    grad_activated = jnp.dot(upstream, out_weight, preferred_element_type=jnp.float32)
    sigmoid_value = jax.nn.sigmoid(before)
    grad_before = (grad_activated * sigmoid_value * (1.0 + before * (1.0 - sigmoid_value))).astype(jnp.bfloat16)
    grad_normed = lax.dot_general(grad_before, in_weight, (((1,), (1,)), ((), ())), preferred_element_type=jnp.float32)
    grad_scaled = grad_normed * norm_gain
    projection = lax.optimization_barrier(jnp.mean(grad_scaled * widened, axis=-1, keepdims=True))
    grad_hidden = upstream.astype(jnp.float32) + inverse * grad_scaled - widened * (inverse * inverse * inverse) * projection
    gain_terms = lax.optimization_barrier(jnp.sum(grad_normed * widened * inverse, axis=0))
    return (grad_hidden.astype(jnp.bfloat16), grad_before, gain_terms)

def replica_sum(left, right, grad_scale):
    left_parts = left.reshape(MICRO, N_REP, TOK_MB, left.shape[-1])
    right_parts = right.reshape(MICRO, N_REP, TOK_MB, right.shape[-1])

    def add_one(total, replica):
        left_rows = lax.dynamic_index_in_dim(left_parts, replica, 1, keepdims=False).reshape(MICRO * TOK_MB, left.shape[-1])
        right_rows = lax.dynamic_index_in_dim(right_parts, replica, 1, keepdims=False).reshape(MICRO * TOK_MB, right.shape[-1])
        term = lax.dot_general(left_rows, right_rows, (((0,), (0,)), ((), ())), preferred_element_type=jnp.float32) * grad_scale
        rounded = lax.optimization_barrier(term.astype(jnp.bfloat16)).astype(jnp.float32)
        return (total + rounded, None)
    start_total = jnp.zeros((left.shape[-1], right.shape[-1]), jnp.float32)
    total, unused = lax.scan(add_one, start_total, jnp.arange(N_REP, dtype=jnp.int32))
    return total.astype(jnp.bfloat16)

def reference(inputs, cotangent, in_weight, out_weight, norm_gain, lengths):
    row_total = MICRO * BATCH_ROWS
    grad_scale = 1.0 / math.sqrt(ALL_ROWS)
    hidden = inputs.reshape(row_total, D)
    saved = []
    for section_index in range(N_SECTION):
        leaving, normed, before, activated = section_forward(hidden, norm_gain[section_index], in_weight[section_index], out_weight[section_index])
        saved.append((hidden, normed, before, activated))
        hidden = leaving
    position = jnp.arange(TOK_MB, dtype=jnp.int32)
    keep_rows = position[None, None, :] < jnp.transpose(lengths)[:, :, None]
    upstream = jnp.where(keep_rows.reshape(row_total, 1), cotangent.reshape(row_total, D), jnp.zeros((), jnp.bfloat16))
    grads_in = [None] * N_SECTION
    grads_out = [None] * N_SECTION
    grads_gain = [None] * N_SECTION
    grads_hidden = [None] * N_SECTION
    for section_index in reversed(range(N_SECTION)):
        hidden, normed, before, activated = saved[section_index]
        grad_hidden, grad_before, gain_terms = section_backward(hidden, norm_gain[section_index], in_weight[section_index], out_weight[section_index], before, upstream)
        grads_in[section_index] = replica_sum(normed, grad_before, grad_scale)
        grads_out[section_index] = replica_sum(upstream, activated, grad_scale)
        grads_gain[section_index] = gain_terms * grad_scale
        grads_hidden[section_index] = grad_hidden.reshape(MICRO, BATCH_ROWS, D)
        upstream = grad_hidden
    return (jnp.stack(grads_in), jnp.stack(grads_out), jnp.stack(grads_gain), jnp.stack(grads_hidden))
```

```python
import math

import jax
import jax.numpy as jnp
import numpy as np
from jax import lax
from jax.sharding import Mesh
from jax.sharding import PartitionSpec as P

norm_epsilon = 1e-05
f32 = jnp.float32
bf16 = jnp.bfloat16

AXES = ("sx", "sy", "z", "xh", "core")
SIZES = (2, 4, 8, 2, 2)
SECTION = ("sx", "sy")
REP = ("z", "xh", "core")
PLANE = ("sx", "sy", "xh")


def exchange(blocks, axes):
    return lax.all_to_all(blocks, axes, 0, 0)


def spread(block, axes):
    count = math.prod(SIZES[AXES.index(axis)] for axis in axes)
    return exchange(jnp.broadcast_to(block[None], (count,) + block.shape), axes)


def block_number(row, column):
    return column * (column + 1) // 2 + row


def recursion(products, energy, gram, width, sections, rank):
    def gram_block(row, column):
        at = 2 * rank * block_number(row, column)
        return gram[:, at : at + 2 * rank]

    activated, before, inverse, outward = [], [], [], []
    for s in range(sections):
        at = 3 * rank * s
        total = products[:, at : at + 2 * rank]
        for t in range(s):
            total = total + jnp.dot(activated[t], gram_block(t, s), preferred_element_type=f32)
        inverse_s = lax.rsqrt(energy / width + norm_epsilon)
        before_s = total[:, :rank] * inverse_s
        activated_s = jax.nn.silu(before_s)
        rounded = activated_s.astype(bf16)
        along = total[:, rank:]
        moved = along + jnp.dot(rounded, gram_block(s, s)[:, rank:], preferred_element_type=f32)
        energy = energy + jnp.sum(rounded.astype(f32) * (along + moved), axis=-1, keepdims=True)
        activated.append(rounded)
        before.append(before_s)
        inverse.append(inverse_s)
        outward.append(moved)
    pulls, shares = [None] * sections, [None] * sections
    later = jnp.zeros_like(energy)
    mixes = [None] * sections
    for s in reversed(range(sections)):
        at = 3 * rank * s + 2 * rank
        grad = products[:, at : at + rank] - later * outward[s]
        for t in range(s + 1, sections):
            grad = grad + lax.dot_general(
                mixes[t], gram_block(s, t), (((1,), (1,)), ((), ())), preferred_element_type=f32
            )
        sigmoid_value = jax.nn.sigmoid(before[s])
        grad_before = grad * sigmoid_value * (1.0 + before[s] * (1.0 - sigmoid_value))
        share = (
            inverse[s] * inverse[s] * jnp.sum(grad_before * before[s], axis=-1, keepdims=True) / width
        )
        pulls[s] = (inverse[s] * grad_before).astype(bf16)
        shares[s] = share
        mixes[s] = jnp.concatenate(
            (pulls[s], (-later * activated[s].astype(f32)).astype(bf16)), axis=1
        )
        later = later + share
    return activated, pulls, shares


def body(inputs, cotangent, in_weight, out_weight, norm_gain, lengths):
    micro_count, tok_rows, width = inputs.shape
    feature_rows, rank = in_weight.shape[1:]
    sections, planes = SIZES[0] * SIZES[1], SIZES[2]
    rows = micro_count * tok_rows
    part = rows // sections
    slab = width // planes
    grad_scale = 1.0 / math.sqrt(width_rows(micro_count, tok_rows))
    section = lax.axis_index(SECTION)
    replica = lax.axis_index(REP)

    gain = lax.dynamic_slice(norm_gain[0], (replica * feature_rows,), (feature_rows,))
    scaled_in = (in_weight[0].astype(f32) * gain[:, None]).astype(bf16)
    own = jnp.concatenate((scaled_in, out_weight[0]), axis=1)
    around = spread(own, PLANE)
    both = spread(around, ("core",))
    weights = both.reshape(2, sections, 2, feature_rows, 2 * rank)
    weights = jnp.transpose(weights, (1, 2, 0, 3, 4)).reshape(sections, slab, 2 * rank)

    own_hidden = lax.dynamic_slice(inputs.reshape(rows, width), (part * section, 0), (part, width))
    own_seed = lax.dynamic_slice(cotangent.reshape(rows, width), (part * section, 0), (part, width))
    numbers = part * section + jnp.arange(part, dtype=jnp.int32)
    micro, place = numbers // tok_rows, numbers % tok_rows
    limit = jnp.sum(
        jnp.where(micro[:, None] == jnp.arange(micro_count)[None, :], lengths, 0), axis=1
    )
    own_seed = jnp.where((place < limit)[:, None], own_seed, jnp.zeros((), bf16))
    energy = jnp.sum(jnp.square(own_hidden.astype(f32)), axis=-1, keepdims=True)
    pair = jnp.stack((own_hidden, own_seed), axis=0).reshape(2, part, planes, slab)
    pair = exchange(jnp.transpose(pair, (2, 0, 1, 3)), ("z",))
    hidden = pair[:, 0].reshape(rows, slab)
    seed = pair[:, 1].reshape(rows, slab)

    strip = lax.axis_index(PLANE) * 2 + lax.axis_index("core")
    few = rank // 32
    picked = strip * few + jnp.arange(few, dtype=jnp.int32)
    chooser = (picked[:, None] == jnp.arange(rank)[None, :]).astype(bf16)
    left = lax.dot_general(
        chooser, weights[:, :, rank:], (((1,), (2,)), ((), ())), preferred_element_type=f32
    ).astype(bf16)
    blocks = []
    for t in range(sections):
        found = lax.dot_general(
            left[:, : t + 1], weights[t], (((2,), (0,)), ((), ())), preferred_element_type=f32
        )
        blocks.append(found.astype(bf16))
    gram = jnp.concatenate(blocks, axis=1)
    gram = jnp.sum(exchange(gram, ("z",)).astype(f32), axis=0).astype(bf16)
    gram = spread(gram, ("z",))
    gram = lax.all_gather(gram, PLANE + ("core",), axis=0, tiled=True)
    gram = gram.reshape(rank, -1)

    pieces = []
    for s in range(sections):
        pieces.append(jnp.dot(hidden, weights[s], preferred_element_type=f32).astype(bf16))
        pieces.append(jnp.dot(seed, weights[s][:, rank:], preferred_element_type=f32).astype(bf16))
    products = jnp.concatenate(pieces, axis=1).reshape(planes, part, 3 * rank * sections)
    products = jnp.sum(exchange(products, ("z",)).astype(f32), axis=0)

    activated, pulls, shares = recursion(products, energy, gram, width, sections, rank)

    shares = jnp.concatenate(shares, axis=1)
    shares_high = shares.astype(bf16)
    shares_low = (shares - shares_high.astype(f32)).astype(bf16)
    filler = jnp.zeros((part, 128 - 2 * sections), bf16)
    found = jnp.concatenate(activated + pulls + [shares_high, shares_low, filler], axis=1)
    found = spread(found, ("z",)).reshape(rows, -1)
    shares = found[:, 2 * rank * sections :].astype(f32)
    shares = shares[:, :sections] + shares[:, sections : 2 * sections]

    states = [hidden.astype(f32)]
    for s in range(sections - 1):
        act = found[:, rank * s : rank * (s + 1)]
        states.append(
            states[-1]
            + lax.dot_general(
                act, weights[s][:, rank:], (((1,), (1,)), ((), ())), preferred_element_type=f32
            )
        )
    upstream = seed.astype(f32)
    grads, uppers = [None] * sections, [None] * sections
    for s in reversed(range(sections)):
        act = found[:, rank * s : rank * (s + 1)]
        pull = found[:, rank * (sections + s) : rank * (sections + s + 1)]
        first = lax.dot_general(
            states[s].astype(bf16), pull, (((0,), (0,)), ((), ())), preferred_element_type=f32
        )
        second = lax.dot_general(
            upstream.astype(bf16), act, (((0,), (0,)), ((), ())), preferred_element_type=f32
        )
        grads[s] = (jnp.concatenate((first, second), axis=1) * grad_scale).astype(bf16)
        upstream = (
            upstream
            + lax.dot_general(
                pull, weights[s][:, :rank], (((1,), (1,)), ((), ())), preferred_element_type=f32
            )
            - shares[:, s : s + 1] * states[s]
        )
        uppers[s] = upstream.astype(bf16)

    uppers = jnp.stack(uppers).reshape(sections, planes, part, slab)
    uppers = exchange(uppers.reshape(sections * planes, part, slab), SECTION + ("z",))
    uppers = uppers.reshape(sections, planes, part, slab)
    grad_inputs = jnp.transpose(uppers, (0, 2, 1, 3)).reshape(1, micro_count, tok_rows, width)

    grads = jnp.stack(grads).reshape(sections, 2, 2, feature_rows, 2 * rank)
    grads = jnp.transpose(grads, (2, 0, 1, 3, 4))
    grads = jnp.sum(exchange(grads, ("core",)).astype(f32), axis=0).astype(bf16)
    grads = grads.reshape(2 * sections, feature_rows, 2 * rank)
    grads = jnp.sum(exchange(grads, PLANE).astype(f32), axis=0)
    raw_in = grads[:, :rank]
    grad_in_weight = (raw_in * gain[:, None]).astype(bf16)[None]
    grad_out_weight = grads[:, rank:].astype(bf16)[None]
    gain_part = jnp.sum(raw_in * in_weight[0].astype(f32), axis=1)
    grad_gain = spread(gain_part, REP).reshape(1, width)
    return (grad_in_weight, grad_out_weight, grad_gain, grad_inputs)


def width_rows(micro_count, tok_rows):
    return micro_count * tok_rows * SIZES[2] * SIZES[3] * SIZES[4]


def solution(mesh):
    fine = Mesh(np.asarray(mesh.devices).reshape(SIZES), AXES)
    in_specs = (
        P(None, REP, None),
        P(None, REP, None),
        P(SECTION, REP, None),
        P(SECTION, REP, None),
        P(SECTION, None),
        P(REP, None),
    )
    out_specs = (
        P(SECTION, REP, None),
        P(SECTION, REP, None),
        P(SECTION, None),
        P(SECTION, None, REP, None),
    )
    return jax.shard_map(body, mesh=fine, in_specs=in_specs, out_specs=out_specs, check_vma=False)
```

```python
import functools
import math

import jax
import jax.numpy as jnp
import numpy as np
from jax import lax
from jax.experimental import pallas as pl
from jax.experimental.pallas import tpu as pltpu
from jax.sharding import Mesh
from jax.sharding import PartitionSpec as P

norm_epsilon = 1e-05
f32 = jnp.float32
bf16 = jnp.bfloat16

AXES = ("sx", "sy", "z", "xh", "core")
SIZES = (2, 4, 8, 2, 2)
SECTION = ("sx", "sy")
REP = ("z", "xh", "core")
X_RING = ("sx", "xh")
Y_RING = ("sy",)


def exchange(blocks, axes):
    return lax.all_to_all(blocks, axes, 0, 0)


def spread(block, axes):
    count = math.prod(SIZES[AXES.index(axis)] for axis in axes)
    return exchange(jnp.broadcast_to(block[None], (count,) + block.shape), axes)


def shifted(block, axes, distance):
    return lax.ppermute(block, axes, [(i, (i + distance) % 4) for i in range(4)])


def put(holder, content, number, dim):
    return lax.dynamic_update_slice_in_dim(holder, jnp.expand_dims(content, dim), number, dim)


def take(holder, number, dim):
    return lax.dynamic_index_in_dim(holder, number, dim, keepdims=False)


def gather_ring(block, axes, dim):
    me = lax.axis_index(axes)
    shape = block.shape[:dim] + (4,) + block.shape[dim:]
    holder = put(jnp.zeros(shape, block.dtype), block, me, dim)
    for distance in (1, 2, 3):
        holder = put(holder, shifted(block, axes, distance), (me - distance) % 4, dim)
    return holder


def gather_plane(first, second):
    return (
        gather_ring(gather_ring(first, X_RING, 0), Y_RING, 0),
        gather_ring(gather_ring(second, Y_RING, 0), X_RING, 1),
    )


def gather_core(block, dim):
    me = lax.axis_index("core")
    shape = block.shape[:dim] + (2,) + block.shape[dim:]
    holder = put(jnp.zeros(shape, block.dtype), block, me, dim)
    other = lax.ppermute(block, "core", [(0, 1), (1, 0)])
    return put(holder, other, 1 - me, dim)


def sum_ring(blocks, axes, dim):
    me = lax.axis_index(axes)
    total = take(blocks, me, dim).astype(f32)
    for distance in (1, 2, 3):
        leaving = take(blocks, (me + distance) % 4, dim)
        total = total + shifted(leaving, axes, distance).astype(f32)
    return total


def sum_plane(first, second):
    first = sum_ring(first, Y_RING, 0).astype(bf16)
    second = sum_ring(second, X_RING, 1).astype(bf16)
    return sum_ring(first, X_RING, 0), sum_ring(second, Y_RING, 0)


def recursion_kernel(width, sections, rank, products, energy_in, low, high, results):
    def unit(number):
        holder, number = (low, number) if number < 32 else (high, number - 32)
        return holder[number // 8, :, (number % 8) * rank : (number % 8 + 1) * rank]

    def dot(left, right):
        return jnp.dot(left, right, preferred_element_type=f32)

    def dot_turned(left, right):
        return lax.dot_general(left, right, (((1,), (1,)), ((), ())), preferred_element_type=f32)

    energy = energy_in[...]
    activated, before, inverse, outward = [], [], [], []
    for s in range(sections):
        at = 3 * rank * s
        total = products[:, at : at + rank]
        along = products[:, at + rank : at + 2 * rank]
        for t in range(s):
            total = total + dot(activated[t], unit(s * s + 2 * t))
            along = along + dot(activated[t], unit(s * s + 2 * t + 1))
        inverse_s = lax.rsqrt(energy / width + norm_epsilon)
        before_s = total * inverse_s
        activated_s = before_s * jax.nn.sigmoid(before_s)
        rounded = activated_s.astype(bf16)
        moved = along + dot(rounded, unit(s * s + 2 * s))
        energy = energy + jnp.sum(rounded.astype(f32) * (along + moved), axis=-1, keepdims=True)
        results[:, rank * s : rank * (s + 1)] = rounded.astype(f32)
        activated.append(rounded)
        before.append(before_s)
        inverse.append(inverse_s)
        outward.append(moved)
    pulls, drags = [None] * sections, [None] * sections
    later = jnp.zeros_like(energy)
    lanes = lax.broadcasted_iota(jnp.int32, (energy.shape[0], 128), 1)
    shares = jnp.zeros((energy.shape[0], 128), f32)
    for s in reversed(range(sections)):
        at = 3 * rank * s + 2 * rank
        grad = products[:, at : at + rank] - later * outward[s]
        for t in range(s + 1, sections):
            grad = grad + dot_turned(pulls[t], unit(t * t + 2 * s))
            grad = grad + dot_turned(drags[t], unit(t * t + 2 * s + 1))
        sigmoid_value = jax.nn.sigmoid(before[s])
        grad_before = grad * sigmoid_value * (1.0 + before[s] * (1.0 - sigmoid_value))
        share = (
            inverse[s] * inverse[s] * jnp.sum(grad_before * before[s], axis=-1, keepdims=True) / width
        )
        pull = inverse[s] * grad_before
        results[:, rank * (sections + s) : rank * (sections + s + 1)] = pull
        pulls[s] = pull.astype(bf16)
        drags[s] = (-later * activated[s].astype(f32)).astype(bf16)
        shares = jnp.where(lanes == s, share, shares)
        later = later + share
    results[:, 2 * rank * sections :] = shares


def recursion(products, energy, low, high, width, sections, rank):
    part = products.shape[0]
    outer = 2 * rank * sections + 128
    return pl.pallas_call(
        functools.partial(recursion_kernel, width, sections, rank),
        out_shape=jax.ShapeDtypeStruct((part, outer), f32),
        in_specs=[pl.BlockSpec(memory_space=pltpu.VMEM)] * 4,
        out_specs=pl.BlockSpec(memory_space=pltpu.VMEM),
        compiler_params=pltpu.CompilerParams(vmem_limit_bytes=32 << 20),
        cost_estimate=pl.CostEstimate(
            flops=2 * part * rank * rank * 120,
            bytes_accessed=2 * (low.size + high.size) + 4 * (products.size + part * outer),
            transcendentals=2 * part * rank * sections,
        ),
    )(products, energy, low, high)


def body(inputs, cotangent, in_weight, out_weight, norm_gain, lengths):
    micro_count, tok_rows, width = inputs.shape
    feature_rows, rank = in_weight.shape[1:]
    sections, planes = SIZES[0] * SIZES[1], SIZES[2]
    rows = micro_count * tok_rows
    part = rows // sections
    slab = width // planes
    grad_scale = 1.0 / math.sqrt(width_rows(micro_count, tok_rows))
    section = lax.axis_index(SECTION)
    replica = lax.axis_index(REP)

    gain = lax.dynamic_slice(norm_gain[0], (replica * feature_rows,), (feature_rows,))
    scaled_in = (in_weight[0].astype(f32) * gain[:, None]).astype(bf16)
    own = jnp.concatenate((scaled_in, out_weight[0]), axis=1)
    half = feature_rows // 2
    halves = gather_plane(own[:half], own[half:])
    halves = jnp.stack([x.reshape(4, 2, 2, half, 2 * rank) for x in halves], axis=3)
    mine = jnp.transpose(halves, (1, 0, 2, 3, 4, 5)).reshape(sections, 2, feature_rows, 2 * rank)
    weights = gather_core(mine, 2).reshape(sections, slab, 2 * rank)

    own_hidden = lax.dynamic_slice(inputs.reshape(rows, width), (part * section, 0), (part, width))
    own_seed = lax.dynamic_slice(cotangent.reshape(rows, width), (part * section, 0), (part, width))
    numbers = part * section + jnp.arange(part, dtype=jnp.int32)
    micro, place = numbers // tok_rows, numbers % tok_rows
    limit = jnp.sum(
        jnp.where(micro[:, None] == jnp.arange(micro_count)[None, :], lengths, 0), axis=1
    )
    own_seed = jnp.where((place < limit)[:, None], own_seed, jnp.zeros((), bf16))
    energy = jnp.sum(jnp.square(own_hidden.astype(f32)), axis=-1, keepdims=True)
    pair = jnp.stack((own_hidden, own_seed), axis=0).reshape(2, part, planes, slab)
    pair = exchange(jnp.transpose(pair, (2, 0, 1, 3)), ("z",))
    weights, pair, energy = lax.optimization_barrier((weights, pair, energy))
    hidden = pair[:, 0].reshape(rows, slab)
    seed = pair[:, 1].reshape(rows, slab)

    x_place, y_place = lax.axis_index(X_RING), lax.axis_index(Y_RING)
    strip = (lax.axis_index("core") * 4 + y_place) * 4 + x_place
    few = rank // 32
    picked = strip * few + jnp.arange(few, dtype=jnp.int32)
    chooser = (picked[:, None] == jnp.arange(rank)[None, :]).astype(bf16)
    left = lax.dot_general(
        weights[:, :, rank:], chooser, (((2,), (1,)), ((), ())), preferred_element_type=f32
    ).astype(bf16)
    left = jnp.transpose(left, (0, 2, 1)).reshape(sections * few, slab)
    units = []
    for t in range(sections):
        found = jnp.dot(left[: few * (t + 1)], weights[t], preferred_element_type=f32)
        for s in range(t):
            units.append(found[few * s : few * (s + 1)])
        units.append(found[few * t :, rank:])
    gram = jnp.concatenate(units, axis=1).astype(bf16)
    gram = jnp.transpose(gram.reshape(few, planes, -1), (1, 0, 2))
    gram = jnp.sum(exchange(gram, ("z",)).astype(f32), axis=0).astype(bf16)
    gram = spread(gram, ("z",))
    low, high = gather_plane(gram[: planes // 2], gram[planes // 2 :])
    low = gather_core(low, 0)
    high = gather_core(high, 0)
    low, high = (
        jnp.transpose(x, (3, 0, 1, 2, 4, 5)).reshape(planes // 2, rank, -1) for x in (low, high)
    )

    pieces = []
    for s in range(sections):
        pieces.append(jnp.dot(hidden, weights[s], preferred_element_type=f32).astype(bf16))
        pieces.append(jnp.dot(seed, weights[s][:, rank:], preferred_element_type=f32).astype(bf16))
    products = jnp.concatenate(pieces, axis=1).reshape(planes, part, 3 * rank * sections)
    products = jnp.sum(exchange(products, ("z",)).astype(f32), axis=0)

    found = recursion(products, energy, low, high, width, sections, rank)
    shares = found[:, 2 * rank * sections : 2 * rank * sections + sections]
    shares_high = shares.astype(bf16)
    shares_low = (shares - shares_high.astype(f32)).astype(bf16)
    filler = jnp.zeros((part, 128 - 2 * sections), bf16)
    found = jnp.concatenate(
        [found[:, : 2 * rank * sections].astype(bf16), shares_high, shares_low, filler], axis=1
    )
    found = spread(found, ("z",)).reshape(rows, -1)
    shares = found[:, 2 * rank * sections :].astype(f32)
    shares = shares[:, :sections] + shares[:, sections : 2 * sections]

    states = [hidden.astype(f32)]
    for s in range(sections - 1):
        act = found[:, rank * s : rank * (s + 1)]
        states.append(
            states[-1]
            + lax.dot_general(
                act, weights[s][:, rank:], (((1,), (1,)), ((), ())), preferred_element_type=f32
            )
        )
    upstream = seed.astype(f32)
    grads, uppers = [None] * sections, [None] * sections
    for s in reversed(range(sections)):
        act = found[:, rank * s : rank * (s + 1)]
        pull = found[:, rank * (sections + s) : rank * (sections + s + 1)]
        first = lax.dot_general(
            states[s].astype(bf16), pull, (((0,), (0,)), ((), ())), preferred_element_type=f32
        )
        second = lax.dot_general(
            upstream.astype(bf16), act, (((0,), (0,)), ((), ())), preferred_element_type=f32
        )
        grads[s] = (jnp.concatenate((first, second), axis=1) * grad_scale).astype(bf16)
        upstream = (
            upstream
            + lax.dot_general(
                pull, weights[s][:, :rank], (((1,), (1,)), ((), ())), preferred_element_type=f32
            )
            - shares[:, s : s + 1] * states[s]
        )
        uppers[s] = upstream.astype(bf16)

    uppers = jnp.stack(uppers).reshape(sections, planes, part, slab)
    uppers = exchange(uppers.reshape(sections * planes, part, slab), SECTION + ("z",))
    uppers = uppers.reshape(sections, planes, part, slab)
    grad_inputs = jnp.transpose(uppers, (0, 2, 1, 3)).reshape(1, micro_count, tok_rows, width)

    grads = jnp.stack(grads).reshape(2, 4, 2, 2, feature_rows, 2 * rank)
    core = lax.axis_index("core")
    kept = take(grads, core, 3)
    other = lax.ppermute(take(grads, 1 - core, 3), "core", [(0, 1), (1, 0)])
    grads = (kept.astype(f32) + other.astype(f32)).astype(bf16)
    grads = jnp.transpose(grads, (1, 0, 2, 3, 4)).reshape(4, 4, feature_rows, 2 * rank)
    grads = jnp.concatenate(sum_plane(grads[:, :, :half], grads[:, :, half:]), axis=0)
    raw_in = grads[:, :rank]
    grad_in_weight = (raw_in * gain[:, None]).astype(bf16)[None]
    grad_out_weight = grads[:, rank:].astype(bf16)[None]
    gain_part = jnp.sum(raw_in * in_weight[0].astype(f32), axis=1)
    grad_gain = spread(gain_part, REP).reshape(1, width)
    return (grad_in_weight, grad_out_weight, grad_gain, grad_inputs)


def width_rows(micro_count, tok_rows):
    return micro_count * tok_rows * SIZES[2] * SIZES[3] * SIZES[4]


def solution(mesh):
    fine = Mesh(np.asarray(mesh.devices).reshape(SIZES), AXES)
    in_specs = (
        P(None, REP, None),
        P(None, REP, None),
        P(SECTION, REP, None),
        P(SECTION, REP, None),
        P(SECTION, None),
        P(REP, None),
    )
    out_specs = (
        P(SECTION, REP, None),
        P(SECTION, REP, None),
        P(SECTION, None),
        P(SECTION, None, REP, None),
    )
    return jax.shard_map(body, mesh=fine, in_specs=in_specs, out_specs=out_specs, check_vma=False)
```

```python
import functools
import math

import jax
import jax.numpy as jnp
import numpy as np
from jax import lax
from jax.experimental import pallas as pl
from jax.experimental.pallas import tpu as pltpu
from jax.sharding import Mesh
from jax.sharding import PartitionSpec as P

norm_epsilon = 1e-05
f32 = jnp.float32
bf16 = jnp.bfloat16

AXES = ("sx", "sy", "z", "xh", "core")
SIZES = (2, 4, 8, 2, 2)
SECTION = ("sx", "sy")
REP = ("z", "xh", "core")
X_RING = ("sx", "xh")
Y_RING = ("sy",)


def exchange(blocks, axes):
    return lax.all_to_all(blocks, axes, 0, 0)


def spread(block, axes):
    count = math.prod(SIZES[AXES.index(axis)] for axis in axes)
    return exchange(jnp.broadcast_to(block[None], (count,) + block.shape), axes)


def shifted(block, axes, distance):
    return lax.ppermute(block, axes, [(i, (i + distance) % 4) for i in range(4)])


def put(holder, content, number, dim):
    return lax.dynamic_update_slice_in_dim(holder, jnp.expand_dims(content, dim), number, dim)


def take(holder, number, dim):
    return lax.dynamic_index_in_dim(holder, number, dim, keepdims=False)


def gather_ring(block, axes, dim):
    me = lax.axis_index(axes)
    shape = block.shape[:dim] + (4,) + block.shape[dim:]
    holder = put(jnp.zeros(shape, block.dtype), block, me, dim)
    for distance in (1, 2, 3):
        holder = put(holder, shifted(block, axes, distance), (me - distance) % 4, dim)
    return holder


def gather_plane(first, second, dim):
    return (
        gather_ring(gather_ring(first, X_RING, dim), Y_RING, dim),
        gather_ring(gather_ring(second, Y_RING, dim), X_RING, dim + 1),
    )


def swap_core(block):
    return lax.ppermute(block, "core", [(0, 1), (1, 0)])


def gather_pair(block, axis):
    me = lax.axis_index(axis)
    holder = put(jnp.zeros((2,) + block.shape, block.dtype), block, me, 0)
    return put(holder, lax.ppermute(block, axis, [(0, 1), (1, 0)]), 1 - me, 0)


def gather_z(block):
    count, me = SIZES[2], lax.axis_index("z")
    holder = put(jnp.zeros((count,) + block.shape, block.dtype), block, me, 0)
    up, down = block, block
    for distance in range(1, count // 2 + 1):
        up = lax.ppermute(up, "z", [(i, (i + 1) % count) for i in range(count)])
        holder = put(holder, up, (me - distance) % count, 0)
        if distance < count // 2:
            down = lax.ppermute(down, "z", [(i, (i - 1) % count) for i in range(count)])
            holder = put(holder, down, (me + distance) % count, 0)
    return holder


def sum_ring(blocks, axes, dim):
    me = lax.axis_index(axes)
    total = take(blocks, me, dim).astype(f32)
    for distance in (1, 2, 3):
        leaving = take(blocks, (me + distance) % 4, dim)
        total = total + shifted(leaving, axes, distance).astype(f32)
    return total


def sum_plane(first, second):
    first = sum_ring(first, Y_RING, 0).astype(bf16)
    second = sum_ring(second, X_RING, 1).astype(bf16)
    return sum_ring(first, X_RING, 0), sum_ring(second, Y_RING, 0)


def dot(left, right):
    return jnp.dot(left, right, preferred_element_type=f32)


def dot_turned(left, right):
    return lax.dot_general(left, right, (((1,), (1,)), ((), ())), preferred_element_type=f32)


def dot_rows(left, right):
    return lax.dot_general(left, right, (((0,), (0,)), ((), ())), preferred_element_type=f32)


def call(kernel, outs, inputs, scalars, scratch, flops):
    spaces = [pltpu.SMEM] * scalars + [pltpu.VMEM] * (len(inputs) - scalars)
    nbytes = sum(x.size * x.dtype.itemsize for x in list(inputs) + list(outs))
    return pl.pallas_call(
        kernel,
        out_shape=outs,
        in_specs=[pl.BlockSpec(memory_space=space) for space in spaces],
        out_specs=[pl.BlockSpec(memory_space=pltpu.VMEM) for _ in outs],
        scratch_shapes=scratch,
        compiler_params=pltpu.CompilerParams(vmem_limit_bytes=40 << 20),
        cost_estimate=pl.CostEstimate(flops=flops, bytes_accessed=nbytes, transcendentals=0),
    )(*inputs)


def assemble_kernel(rank, few, core, chooser, mine_a, mine_b, other_a, other_b, weights, gram):
    sections, half = weights.shape[0], mine_a.shape[2]
    for s in range(sections):
        for x_hi in range(2):
            for mine, a, b in ((True, mine_a, mine_b), (False, other_a, other_b)):
                owner = core[0] if mine else 1 - core[0]
                for number, source in ((0, a), (1, b)):
                    at = pl.multiple_of((4 * x_hi + number + 2 * owner) * half, half)
                    weights[s, pl.ds(at, half), :] = source[s % 4, 2 * (s // 4) + x_hi]
    left = [dot_turned(chooser[...], weights[s, :, rank:]) for s in range(sections)]
    left = jnp.concatenate(left, axis=0).astype(bf16)
    for t in range(sections):
        found = dot(left, weights[t])
        for s in range(t + 1):
            for kind in (0, 1) if s < t else (1,):
                unit = t * t + 2 * s + (kind if s < t else 0)
                gram[unit // 8, :, (unit % 8) * rank : (unit % 8 + 1) * rank] = found[
                    few * s : few * (s + 1), kind * rank : (kind + 1) * rank
                ]


def products_kernel(rank, hidden, seed, weights, products):
    planes, part, _ = products.shape
    for s in range(weights.shape[0]):
        at = 3 * rank * s
        plain = dot(hidden[...], weights[s])
        turned = dot(seed[...], weights[s, :, rank:])
        for z in range(planes):
            rows = slice(part * z, part * (z + 1))
            products[z, :, at : at + 2 * rank] = plain[rows].astype(bf16)
            products[z, :, at + 2 * rank : at + 3 * rank] = turned[rows].astype(bf16)


def recursion_kernel(
    width, sections, rank, core, products, energy_in, mine_a, mine_b, other_a, other_b, results
):
    half = rank // 2
    part = products.shape[0]
    lowest = jnp.full((part, half), core[0], jnp.int32) == 0

    def unit(number):
        mine, other = (mine_a, other_a) if number < 32 else (mine_b, other_b)
        number = number % 32
        columns = slice((number % 8) * rank, (number % 8 + 1) * rank)
        return mine[number // 8, :, columns], other[number // 8, :, columns]

    def ordered(low, high):
        return jnp.where(lowest, low, high), jnp.where(lowest, high, low)

    def dot_unit(left, number):
        mine, other = unit(number)
        return dot(left[0], mine) + dot(left[1], other)

    energy = energy_in[...]
    activated, before, inverse, outward = [], [], [], []
    for s in range(sections):
        at = 3 * rank * s
        total = products[:, at : at + rank]
        along = products[:, at + rank : at + 2 * rank]
        for t in range(s):
            total = total + dot_unit(activated[t], s * s + 2 * t)
            along = along + dot_unit(activated[t], s * s + 2 * t + 1)
        inverse_s = lax.rsqrt(energy / width + norm_epsilon)
        before_s = total * inverse_s
        activated_s = before_s * jax.nn.sigmoid(before_s)
        rounded = activated_s.astype(bf16).astype(f32)
        results[:, rank * s : rank * (s + 1)] = rounded
        pieces = [x.astype(bf16) for x in ordered(rounded[:, :half], rounded[:, half:])]
        moved = along + dot_unit(pieces, s * s + 2 * s)
        energy = energy + jnp.sum(rounded * (along + moved), axis=-1, keepdims=True)
        activated.append(pieces)
        before.append(before_s)
        inverse.append(inverse_s)
        outward.append(moved)
    pulls, drags = [None] * sections, [None] * sections
    later = jnp.zeros_like(energy)
    lanes = lax.broadcasted_iota(jnp.int32, (part, 128), 1)
    shares = jnp.zeros((part, 128), f32)
    for s in reversed(range(sections)):
        at = 3 * rank * s + 2 * rank
        grad = products[:, at : at + rank] - later * outward[s]
        if s < sections - 1:
            gained, gained_other = jnp.zeros((part, half), f32), jnp.zeros((part, half), f32)
            for t in range(s + 1, sections):
                for left, number in ((pulls[t], t * t + 2 * s), (drags[t], t * t + 2 * s + 1)):
                    mine, other = unit(number)
                    gained = gained + dot_turned(left, mine)
                    gained_other = gained_other + dot_turned(left, other)
            grad = grad + jnp.concatenate(ordered(gained, gained_other), axis=1)
        sigmoid_value = jax.nn.sigmoid(before[s])
        grad_before = grad * sigmoid_value * (1.0 + before[s] * (1.0 - sigmoid_value))
        share = (
            inverse[s] * inverse[s] * jnp.sum(grad_before * before[s], axis=-1, keepdims=True) / width
        )
        pull = inverse[s] * grad_before
        results[:, rank * (sections + s) : rank * (sections + s + 1)] = pull
        pulls[s] = pull.astype(bf16)
        drags[s] = (-later * results[:, rank * s : rank * (s + 1)]).astype(bf16)
        shares = jnp.where(lanes == s, share, shares)
        later = later + share
    results[:, 2 * rank * sections :] = shares


def wide_kernel(rank, grad_scale, hidden, seed, found, weights, uppers, grads, states):
    sections, planes, part, _ = uppers.shape
    half = grads.shape[4]
    tail = found[:, 2 * rank * sections :].astype(f32)
    state = hidden[...].astype(f32)
    states[0] = state
    for s in range(sections - 1):
        state = state + dot_turned(found[:, rank * s : rank * (s + 1)], weights[s, :, rank:])
        states[s + 1] = state
    upstream = seed[...].astype(f32)
    for s in reversed(range(sections)):
        act = found[:, rank * s : rank * (s + 1)]
        pull = found[:, rank * (sections + s) : rank * (sections + s + 1)]
        first = (dot_rows(states[s].astype(bf16), pull) * grad_scale).astype(bf16)
        second = (dot_rows(upstream.astype(bf16), act) * grad_scale).astype(bf16)
        for x_hi in range(2):
            for core in range(2):
                for number in range(2):
                    at = (4 * x_hi + 2 * core + number) * half
                    place = (core, number, s % 4, 2 * (s // 4) + x_hi)
                    grads[place + (slice(None), slice(0, rank))] = first[at : at + half]
                    grads[place + (slice(None), slice(rank, 2 * rank))] = second[at : at + half]
        share = tail[:, s : s + 1] + tail[:, sections + s : sections + s + 1]
        upstream = upstream + dot_turned(pull, weights[s, :, :rank]) - share * states[s]
        for z in range(planes):
            uppers[s, z] = upstream[part * z : part * (z + 1)].astype(bf16)


def body(inputs, cotangent, in_weight, out_weight, norm_gain, lengths):
    micro_count, tok_rows, width = inputs.shape
    feature_rows, rank = in_weight.shape[1:]
    sections, planes = SIZES[0] * SIZES[1], SIZES[2]
    rows = micro_count * tok_rows
    part = rows // sections
    slab = width // planes
    grad_scale = 1.0 / math.sqrt(width_rows(micro_count, tok_rows))
    section = lax.axis_index(SECTION)
    replica = lax.axis_index(REP)

    gain = lax.dynamic_slice(norm_gain[0], (replica * feature_rows,), (feature_rows,))
    scaled_in = (in_weight[0].astype(f32) * gain[:, None]).astype(bf16)
    own = jnp.concatenate((scaled_in, out_weight[0]), axis=1)
    half = feature_rows // 2
    halves = gather_plane(own[:half], own[half:], 0)

    own_hidden = lax.dynamic_slice(inputs.reshape(rows, width), (part * section, 0), (part, width))
    own_seed = lax.dynamic_slice(cotangent.reshape(rows, width), (part * section, 0), (part, width))
    numbers = part * section + jnp.arange(part, dtype=jnp.int32)
    micro, place = numbers // tok_rows, numbers % tok_rows
    limit = jnp.sum(
        jnp.where(micro[:, None] == jnp.arange(micro_count)[None, :], lengths, 0), axis=1
    )
    own_seed = jnp.where((place < limit)[:, None], own_seed, jnp.zeros((), bf16))
    energy = jnp.sum(jnp.square(own_hidden.astype(f32)), axis=-1, keepdims=True)
    pair = jnp.stack((own_hidden, own_seed), axis=0).reshape(2, part, planes, slab)
    pair = exchange(jnp.transpose(pair, (2, 0, 1, 3)), ("z",))
    halves, pair, energy = lax.optimization_barrier((halves, pair, energy))
    others = [swap_core(x) for x in halves]
    hidden = pair[:, 0].reshape(rows, slab)
    seed = pair[:, 1].reshape(rows, slab)

    x_place, y_place = lax.axis_index(X_RING), lax.axis_index(Y_RING)
    strip = (lax.axis_index("core") * 4 + y_place) * 4 + x_place
    few = rank // 32
    picked = strip * few + jnp.arange(few, dtype=jnp.int32)
    chooser = (picked[:, None] == jnp.arange(rank)[None, :]).astype(bf16)
    core = lax.axis_index("core").astype(jnp.int32)[None]
    weights, gram = call(
        functools.partial(assemble_kernel, rank, few),
        (
            jax.ShapeDtypeStruct((sections, slab, 2 * rank), bf16),
            jax.ShapeDtypeStruct((planes, few, sections * rank), f32),
        ),
        (core, chooser, *halves, *others),
        1,
        [],
        2 * sections * sections * few * slab * 2 * rank,
    )
    gram = exchange(gram.astype(bf16), ("z",))
    gram = jnp.sum(gram.astype(f32), axis=0).astype(bf16)
    gram = spread(gram, ("z",))
    grams = gather_plane(gram[: planes // 2], gram[planes // 2 :], 1)
    grams = [x.reshape(planes // 2, rank // 2, -1) for x in grams]
    other_grams = [swap_core(x) for x in grams]

    (products,) = call(
        functools.partial(products_kernel, rank),
        (jax.ShapeDtypeStruct((planes, part, 3 * rank * sections), bf16),),
        (hidden, seed, weights),
        0,
        [],
        2 * rows * slab * 3 * rank * sections,
    )
    products = jnp.sum(exchange(products, ("z",)).astype(f32), axis=0)

    (found,) = call(
        functools.partial(recursion_kernel, width, sections, rank),
        (jax.ShapeDtypeStruct((part, 2 * rank * sections + 128), f32),),
        (core, products, energy, *grams, *other_grams),
        1,
        [],
        2 * part * rank * rank * 120,
    )
    shares = found[:, 2 * rank * sections : 2 * rank * sections + sections]
    shares_high = shares.astype(bf16)
    shares_low = (shares - shares_high.astype(f32)).astype(bf16)
    filler = jnp.zeros((part, 128 - 2 * sections), bf16)
    found = jnp.concatenate(
        [found[:, : 2 * rank * sections].astype(bf16), shares_high, shares_low, filler], axis=1
    )
    found = gather_z(found).reshape(rows, -1)

    uppers, grads = call(
        functools.partial(wide_kernel, rank, grad_scale),
        (
            jax.ShapeDtypeStruct((sections, planes, part, slab), bf16),
            jax.ShapeDtypeStruct((2, 2, 4, 4, half, 2 * rank), bf16),
        ),
        (hidden, seed, found, weights),
        0,
        [pltpu.VMEM((sections, rows, slab), f32)],
        8 * rows * slab * rank * sections,
    )
    uppers = exchange(uppers.reshape(sections * planes, part, slab), SECTION + ("z",))
    uppers = uppers.reshape(sections, planes, part, slab)
    grad_inputs = jnp.transpose(uppers, (0, 2, 1, 3)).reshape(1, micro_count, tok_rows, width)

    me = lax.axis_index("core")
    other = swap_core(take(grads, 1 - me, 0))
    grads = (take(grads, me, 0).astype(f32) + other.astype(f32)).astype(bf16)
    grads = jnp.concatenate(sum_plane(grads[0], grads[1]), axis=0)
    grads, grad_inputs = lax.optimization_barrier((grads, grad_inputs))
    raw_in = grads[:, :rank]
    grad_in_weight = (raw_in * gain[:, None]).astype(bf16)[None]
    grad_out_weight = grads[:, rank:].astype(bf16)[None]
    gain_part = jnp.sum(raw_in * in_weight[0].astype(f32), axis=1)
    gain_part = gather_pair(gather_pair(gain_part[None], "core"), "xh")
    grad_gain = gather_z(gain_part).reshape(1, width)
    return (grad_in_weight, grad_out_weight, grad_gain, grad_inputs)


def width_rows(micro_count, tok_rows):
    return micro_count * tok_rows * SIZES[2] * SIZES[3] * SIZES[4]


def solution(mesh):
    fine = Mesh(np.asarray(mesh.devices).reshape(SIZES), AXES)
    in_specs = (
        P(None, REP, None),
        P(None, REP, None),
        P(SECTION, REP, None),
        P(SECTION, REP, None),
        P(SECTION, None),
        P(REP, None),
    )
    out_specs = (
        P(SECTION, REP, None),
        P(SECTION, REP, None),
        P(SECTION, None),
        P(SECTION, None, REP, None),
    )
    return jax.shard_map(body, mesh=fine, in_specs=in_specs, out_specs=out_specs, check_vma=False)
```

```python
import functools
import math

import jax
import jax.numpy as jnp
import numpy as np
from jax import lax
from jax.experimental import pallas as pl
from jax.experimental.pallas import tpu as pltpu
from jax.sharding import Mesh
from jax.sharding import PartitionSpec as P

norm_epsilon = 1e-05
f32 = jnp.float32
bf16 = jnp.bfloat16

AXES = ("sx", "sy", "z", "xh", "core")
SIZES = (2, 4, 8, 2, 2)
SECTION = ("sx", "sy")
REP = ("z", "xh", "core")
X_RING = ("sx", "xh")
Y_RING = ("sy",)


def exchange(blocks, axes):
    return lax.all_to_all(blocks, axes, 0, 0)


def spread(block, axes):
    count = math.prod(SIZES[AXES.index(axis)] for axis in axes)
    return exchange(jnp.broadcast_to(block[None], (count,) + block.shape), axes)


def shifted(block, axes, distance):
    return lax.ppermute(block, axes, [(i, (i + distance) % 4) for i in range(4)])


def put(holder, content, number, dim):
    return lax.dynamic_update_slice_in_dim(holder, jnp.expand_dims(content, dim), number, dim)


def take(holder, number, dim):
    return lax.dynamic_index_in_dim(holder, number, dim, keepdims=False)


def gather_ring(block, axes, dim):
    me = lax.axis_index(axes)
    shape = block.shape[:dim] + (4,) + block.shape[dim:]
    holder = put(jnp.zeros(shape, block.dtype), block, me, dim)
    for distance in (1, 2, 3):
        holder = put(holder, shifted(block, axes, distance), (me - distance) % 4, dim)
    return holder


def gather_plane(first, second, dim):
    return (
        gather_ring(gather_ring(first, X_RING, dim), Y_RING, dim),
        gather_ring(gather_ring(second, Y_RING, dim), X_RING, dim + 1),
    )


def swap_core(block):
    return lax.ppermute(block, "core", [(0, 1), (1, 0)])


def gather_pair(block, axis):
    me = lax.axis_index(axis)
    holder = put(jnp.zeros((2,) + block.shape, block.dtype), block, me, 0)
    return put(holder, lax.ppermute(block, axis, [(0, 1), (1, 0)]), 1 - me, 0)


def gather_z(block):
    count, me = SIZES[2], lax.axis_index("z")
    holder = put(jnp.zeros((count,) + block.shape, block.dtype), block, me, 0)
    up, down = block, block
    for distance in range(1, count // 2 + 1):
        up = lax.ppermute(up, "z", [(i, (i + 1) % count) for i in range(count)])
        holder = put(holder, up, (me - distance) % count, 0)
        if distance < count // 2:
            down = lax.ppermute(down, "z", [(i, (i - 1) % count) for i in range(count)])
            holder = put(holder, down, (me + distance) % count, 0)
    return holder


def send_z(block, distance):
    count = SIZES[2]
    return lax.ppermute(block, "z", [(i, (i + distance) % count) for i in range(count)])


def gather_direct(block):
    count, me = SIZES[2], lax.axis_index("z")
    holder = put(jnp.zeros((count,) + block.shape, block.dtype), block, me, 0)
    for distance in range(1, count):
        holder = put(holder, send_z(block, distance), (me - distance) % count, 0)
    return holder


def sum_direct(blocks):
    count, me = SIZES[2], lax.axis_index("z")
    total = take(blocks, me, 0).astype(f32)
    for distance in range(1, count):
        total = total + send_z(take(blocks, (me + distance) % count, 0), distance).astype(f32)
    return total


def sum_ring(blocks, axes, dim):
    me = lax.axis_index(axes)
    total = take(blocks, me, dim).astype(f32)
    for distance in (1, 2, 3):
        leaving = take(blocks, (me + distance) % 4, dim)
        total = total + shifted(leaving, axes, distance).astype(f32)
    return total


def sum_plane(first, second):
    first = sum_ring(first, Y_RING, 0).astype(bf16)
    second = sum_ring(second, X_RING, 1).astype(bf16)
    return sum_ring(first, X_RING, 0), sum_ring(second, Y_RING, 0)


def dot(left, right):
    return jnp.dot(left, right, preferred_element_type=f32)


def dot_turned(left, right):
    return lax.dot_general(left, right, (((1,), (1,)), ((), ())), preferred_element_type=f32)


def dot_rows(left, right):
    return lax.dot_general(left, right, (((0,), (0,)), ((), ())), preferred_element_type=f32)


def call(kernel, outs, inputs, scalars, scratch, flops):
    spaces = [pltpu.SMEM] * scalars + [pltpu.VMEM] * (len(inputs) - scalars)
    nbytes = sum(x.size * x.dtype.itemsize for x in list(inputs) + list(outs))
    return pl.pallas_call(
        kernel,
        out_shape=outs,
        in_specs=[pl.BlockSpec(memory_space=space) for space in spaces],
        out_specs=[pl.BlockSpec(memory_space=pltpu.VMEM) for _ in outs],
        scratch_shapes=scratch,
        compiler_params=pltpu.CompilerParams(vmem_limit_bytes=40 << 20),
        cost_estimate=pl.CostEstimate(flops=flops, bytes_accessed=nbytes, transcendentals=0),
    )(*inputs)


def assemble_kernel(rank, few, core, chooser, mine_a, mine_b, other_a, other_b, weights, gram):
    sections, half = weights.shape[0], mine_a.shape[2]
    for s in range(sections):
        for x_hi in range(2):
            for mine, a, b in ((True, mine_a, mine_b), (False, other_a, other_b)):
                owner = core[0] if mine else 1 - core[0]
                for number, source in ((0, a), (1, b)):
                    at = pl.multiple_of((4 * x_hi + number + 2 * owner) * half, half)
                    weights[s, pl.ds(at, half), :] = source[s % 4, 2 * (s // 4) + x_hi]
    left = [dot_turned(chooser[...], weights[s, :, rank:]) for s in range(sections)]
    left = jnp.concatenate(left, axis=0).astype(bf16)
    for t in range(sections):
        found = dot(left, weights[t])
        for s in range(t + 1):
            for kind in (0, 1) if s < t else (1,):
                unit = t * t + 2 * s + (kind if s < t else 0)
                gram[unit // 8, :, (unit % 8) * rank : (unit % 8 + 1) * rank] = found[
                    few * s : few * (s + 1), kind * rank : (kind + 1) * rank
                ]


def products_kernel(rank, hidden, seed, weights, products):
    planes, part, _ = products.shape
    for s in range(weights.shape[0]):
        at = 3 * rank * s
        plain = dot(hidden[...], weights[s])
        turned = dot(seed[...], weights[s, :, rank:])
        for z in range(planes):
            rows = slice(part * z, part * (z + 1))
            products[z, :, at : at + 2 * rank] = plain[rows].astype(bf16)
            products[z, :, at + 2 * rank : at + 3 * rank] = turned[rows].astype(bf16)


def recursion_kernel(
    width, sections, rank, core, products, energy_in, mine_a, mine_b, other_a, other_b, results
):
    half = rank // 2
    part = products.shape[0]
    lowest = jnp.full((part, half), core[0], jnp.int32) == 0

    def unit(number):
        mine, other = (mine_a, other_a) if number < 32 else (mine_b, other_b)
        number = number % 32
        columns = slice((number % 8) * rank, (number % 8 + 1) * rank)
        return mine[number // 8, :, columns], other[number // 8, :, columns]

    def ordered(low, high):
        return jnp.where(lowest, low, high), jnp.where(lowest, high, low)

    def dot_unit(left, number):
        mine, other = unit(number)
        return dot(left[0], mine) + dot(left[1], other)

    energy = energy_in[...]
    activated, before, inverse, outward = [], [], [], []
    for s in range(sections):
        at = 3 * rank * s
        total = products[:, at : at + rank]
        along = products[:, at + rank : at + 2 * rank]
        for t in range(s):
            total = total + dot_unit(activated[t], s * s + 2 * t)
            along = along + dot_unit(activated[t], s * s + 2 * t + 1)
        inverse_s = lax.rsqrt(energy / width + norm_epsilon)
        before_s = total * inverse_s
        activated_s = before_s * jax.nn.sigmoid(before_s)
        rounded = activated_s.astype(bf16).astype(f32)
        results[:, rank * s : rank * (s + 1)] = rounded
        pieces = [x.astype(bf16) for x in ordered(rounded[:, :half], rounded[:, half:])]
        moved = along + dot_unit(pieces, s * s + 2 * s)
        energy = energy + jnp.sum(rounded * (along + moved), axis=-1, keepdims=True)
        activated.append(pieces)
        before.append(before_s)
        inverse.append(inverse_s)
        outward.append(moved)
    pulls, drags = [None] * sections, [None] * sections
    later = jnp.zeros_like(energy)
    lanes = lax.broadcasted_iota(jnp.int32, (part, 128), 1)
    shares = jnp.zeros((part, 128), f32)
    for s in reversed(range(sections)):
        at = 3 * rank * s + 2 * rank
        grad = products[:, at : at + rank] - later * outward[s]
        if s < sections - 1:
            gained, gained_other = jnp.zeros((part, half), f32), jnp.zeros((part, half), f32)
            for t in range(s + 1, sections):
                for left, number in ((pulls[t], t * t + 2 * s), (drags[t], t * t + 2 * s + 1)):
                    mine, other = unit(number)
                    gained = gained + dot_turned(left, mine)
                    gained_other = gained_other + dot_turned(left, other)
            grad = grad + jnp.concatenate(ordered(gained, gained_other), axis=1)
        sigmoid_value = jax.nn.sigmoid(before[s])
        grad_before = grad * sigmoid_value * (1.0 + before[s] * (1.0 - sigmoid_value))
        share = (
            inverse[s] * inverse[s] * jnp.sum(grad_before * before[s], axis=-1, keepdims=True) / width
        )
        pull = inverse[s] * grad_before
        results[:, rank * (sections + s) : rank * (sections + s + 1)] = pull
        pulls[s] = pull.astype(bf16)
        drags[s] = (-later * results[:, rank * s : rank * (s + 1)]).astype(bf16)
        shares = jnp.where(lanes == s, share, shares)
        later = later + share
    results[:, 2 * rank * sections :] = shares


def wide_kernel(rank, grad_scale, hidden, seed, found, weights, uppers, grads, gains, states):
    sections, planes, part, _ = uppers.shape
    half = grads.shape[4]
    tail = found[:, 2 * rank * sections :].astype(f32)
    state = hidden[...].astype(f32)
    states[0] = state
    for s in range(sections - 1):
        state = state + dot_turned(found[:, rank * s : rank * (s + 1)], weights[s, :, rank:])
        states[s + 1] = state
    upstream = seed[...].astype(f32)
    for s in reversed(range(sections)):
        act = found[:, rank * s : rank * (s + 1)]
        pull = found[:, rank * (sections + s) : rank * (sections + s + 1)]
        first = (dot_rows(states[s].astype(bf16), pull) * grad_scale).astype(bf16)
        second = (dot_rows(upstream.astype(bf16), act) * grad_scale).astype(bf16)
        for x_hi in range(2):
            for core in range(2):
                for number in range(2):
                    at = (4 * x_hi + 2 * core + number) * half
                    place = (core, number, s % 4, 2 * (s // 4) + x_hi)
                    grads[place + (slice(None), slice(0, rank))] = first[at : at + half]
                    grads[place + (slice(None), slice(rank, 2 * rank))] = second[at : at + half]
        share = tail[:, s : s + 1] + tail[:, sections + s : sections + s + 1]
        pulled = dot_turned(pull, weights[s, :, :rank])
        gains[s : s + 1, :] = jnp.sum(pulled * states[s], axis=0, keepdims=True) * grad_scale
        upstream = upstream + pulled - share * states[s]
        for z in range(planes):
            uppers[s, z] = upstream[part * z : part * (z + 1)].astype(bf16)


def body(inputs, cotangent, in_weight, out_weight, norm_gain, lengths):
    micro_count, tok_rows, width = inputs.shape
    feature_rows, rank = in_weight.shape[1:]
    sections, planes = SIZES[0] * SIZES[1], SIZES[2]
    rows = micro_count * tok_rows
    part = rows // sections
    slab = width // planes
    grad_scale = 1.0 / math.sqrt(width_rows(micro_count, tok_rows))
    section = lax.axis_index(SECTION)
    replica = lax.axis_index(REP)

    gain = lax.dynamic_slice(norm_gain[0], (replica * feature_rows,), (feature_rows,))
    scaled_in = (in_weight[0].astype(f32) * gain[:, None]).astype(bf16)
    own = jnp.concatenate((scaled_in, out_weight[0]), axis=1)
    half = feature_rows // 2
    started = [gather_ring(own[:half], X_RING, 0), gather_ring(own[half:], Y_RING, 0)]

    own_hidden = lax.dynamic_slice(inputs.reshape(rows, width), (part * section, 0), (part, width))
    own_seed = lax.dynamic_slice(cotangent.reshape(rows, width), (part * section, 0), (part, width))
    numbers = part * section + jnp.arange(part, dtype=jnp.int32)
    micro, place = numbers // tok_rows, numbers % tok_rows
    limit = jnp.sum(
        jnp.where(micro[:, None] == jnp.arange(micro_count)[None, :], lengths, 0), axis=1
    )
    own_seed = jnp.where((place < limit)[:, None], own_seed, jnp.zeros((), bf16))
    energy = jnp.sum(jnp.square(own_hidden.astype(f32)), axis=-1, keepdims=True)
    pair = jnp.stack((own_hidden, own_seed), axis=0).reshape(2, part, planes, slab)
    started, pair = lax.optimization_barrier((started, jnp.transpose(pair, (2, 0, 1, 3))))
    halves = [gather_ring(started[0], Y_RING, 0), gather_ring(started[1], X_RING, 1)]
    pair = exchange(pair, ("z",))
    halves, pair, energy = lax.optimization_barrier((halves, pair, energy))
    others = [swap_core(x) for x in halves]
    hidden = pair[:, 0].reshape(rows, slab)
    seed = pair[:, 1].reshape(rows, slab)

    x_place, y_place = lax.axis_index(X_RING), lax.axis_index(Y_RING)
    strip = (lax.axis_index("core") * 4 + y_place) * 4 + x_place
    few = rank // 32
    picked = strip * few + jnp.arange(few, dtype=jnp.int32)
    chooser = (picked[:, None] == jnp.arange(rank)[None, :]).astype(bf16)
    core = lax.axis_index("core").astype(jnp.int32)[None]
    weights, gram = call(
        functools.partial(assemble_kernel, rank, few),
        (
            jax.ShapeDtypeStruct((sections, slab, 2 * rank), bf16),
            jax.ShapeDtypeStruct((planes, few, sections * rank), f32),
        ),
        (core, chooser, *halves, *others),
        1,
        [],
        2 * sections * sections * few * slab * 2 * rank,
    )
    gram = sum_direct(gram.astype(bf16)).astype(bf16)
    gram = gather_direct(gram)
    grams = gather_plane(gram[: planes // 2], gram[planes // 2 :], 1)
    grams = [x.reshape(planes // 2, rank // 2, -1) for x in grams]
    other_grams = [swap_core(x) for x in grams]

    (products,) = call(
        functools.partial(products_kernel, rank),
        (jax.ShapeDtypeStruct((planes, part, 3 * rank * sections), bf16),),
        (hidden, seed, weights),
        0,
        [],
        2 * rows * slab * 3 * rank * sections,
    )
    products = jnp.sum(exchange(products, ("z",)).astype(f32), axis=0)

    (found,) = call(
        functools.partial(recursion_kernel, width, sections, rank),
        (jax.ShapeDtypeStruct((part, 2 * rank * sections + 128), f32),),
        (core, products, energy, *grams, *other_grams),
        1,
        [],
        2 * part * rank * rank * 120,
    )
    shares = found[:, 2 * rank * sections : 2 * rank * sections + sections]
    shares_high = shares.astype(bf16)
    shares_low = (shares - shares_high.astype(f32)).astype(bf16)
    filler = jnp.zeros((part, 128 - 2 * sections), bf16)
    found = jnp.concatenate(
        [found[:, : 2 * rank * sections].astype(bf16), shares_high, shares_low, filler], axis=1
    )
    found = gather_z(found).reshape(rows, -1)

    uppers, grads, gains = call(
        functools.partial(wide_kernel, rank, grad_scale),
        (
            jax.ShapeDtypeStruct((sections, planes, part, slab), bf16),
            jax.ShapeDtypeStruct((2, 2, 4, 4, half, 2 * rank), bf16),
            jax.ShapeDtypeStruct((sections, slab), f32),
        ),
        (hidden, seed, found, weights),
        0,
        [pltpu.VMEM((sections, rows, slab), f32)],
        8 * rows * slab * rank * sections,
    )
    uppers = exchange(uppers.reshape(sections * planes, part, slab), SECTION + ("z",))
    uppers = uppers.reshape(sections, planes, part, slab)
    grad_inputs = jnp.transpose(uppers, (0, 2, 1, 3)).reshape(1, micro_count, tok_rows, width)

    me = lax.axis_index("core")
    other = swap_core(take(grads, 1 - me, 0))
    grads = (take(grads, me, 0).astype(f32) + other.astype(f32)).astype(bf16)
    grads = jnp.concatenate(sum_plane(grads[0], grads[1]), axis=0)

    gains = gains.reshape(2, 4, slab)
    low = lax.axis_index("sx")
    gains = take(gains, low, 0) + lax.ppermute(take(gains, 1 - low, 0), "sx", [(0, 1), (1, 0)])
    gains = sum_ring(gains[:, None], Y_RING, 0)
    gains = gains + lax.ppermute(gains, "xh", [(0, 1), (1, 0)])
    gains = gains + swap_core(gains)
    grad_gain = gather_direct(gains[0]).reshape(1, width) / norm_gain
    grads, grad_gain, grad_inputs = lax.optimization_barrier((grads, grad_gain, grad_inputs))
    raw_in = grads[:, :rank]
    grad_in_weight = (raw_in * gain[:, None]).astype(bf16)[None]
    grad_out_weight = grads[:, rank:].astype(bf16)[None]
    return (grad_in_weight, grad_out_weight, grad_gain, grad_inputs)


def width_rows(micro_count, tok_rows):
    return micro_count * tok_rows * SIZES[2] * SIZES[3] * SIZES[4]


def solution(mesh):
    fine = Mesh(np.asarray(mesh.devices).reshape(SIZES), AXES)
    in_specs = (
        P(None, REP, None),
        P(None, REP, None),
        P(SECTION, REP, None),
        P(SECTION, REP, None),
        P(SECTION, None),
        P(REP, None),
    )
    out_specs = (
        P(SECTION, REP, None),
        P(SECTION, REP, None),
        P(SECTION, None),
        P(SECTION, None, REP, None),
    )
    return jax.shard_map(body, mesh=fine, in_specs=in_specs, out_specs=out_specs, check_vma=False)
```

```python
import functools
import math

import jax
import jax.numpy as jnp
import numpy as np
from jax import lax
from jax.experimental import pallas as pl
from jax.experimental.pallas import tpu as pltpu
from jax.sharding import Mesh
from jax.sharding import PartitionSpec as P

norm_epsilon = 1e-05
f32 = jnp.float32
bf16 = jnp.bfloat16

AXES = ("sx", "sy", "z", "xh", "core")
SIZES = (2, 4, 8, 2, 2)
SECTION = ("sx", "sy")
REP = ("z", "xh", "core")
X_RING = ("sx", "xh")
Y_RING = ("sy",)


def exchange(blocks, axes):
    return lax.all_to_all(blocks, axes, 0, 0)


def spread(block, axes):
    count = math.prod(SIZES[AXES.index(axis)] for axis in axes)
    return exchange(jnp.broadcast_to(block[None], (count,) + block.shape), axes)


def shifted(block, axes, distance):
    return lax.ppermute(block, axes, [(i, (i + distance) % 4) for i in range(4)])


def put(holder, content, number, dim):
    return lax.dynamic_update_slice_in_dim(holder, jnp.expand_dims(content, dim), number, dim)


def take(holder, number, dim):
    return lax.dynamic_index_in_dim(holder, number, dim, keepdims=False)


def gather_ring(block, axes, dim):
    me = lax.axis_index(axes)
    shape = block.shape[:dim] + (4,) + block.shape[dim:]
    holder = put(jnp.zeros(shape, block.dtype), block, me, dim)
    for distance in (1, 2, 3):
        holder = put(holder, shifted(block, axes, distance), (me - distance) % 4, dim)
    return holder


def gather_plane(first, second, dim):
    return (
        gather_ring(gather_ring(first, X_RING, dim), Y_RING, dim),
        gather_ring(gather_ring(second, Y_RING, dim), X_RING, dim + 1),
    )


def swap_core(block):
    return lax.ppermute(block, "core", [(0, 1), (1, 0)])


def gather_z(block):
    count, me = SIZES[2], lax.axis_index("z")
    holder = put(jnp.zeros((count,) + block.shape, block.dtype), block, me, 0)
    up, down = block, block
    for distance in range(1, count // 2 + 1):
        up = lax.ppermute(up, "z", [(i, (i + 1) % count) for i in range(count)])
        holder = put(holder, up, (me - distance) % count, 0)
        if distance < count // 2:
            down = lax.ppermute(down, "z", [(i, (i - 1) % count) for i in range(count)])
            holder = put(holder, down, (me + distance) % count, 0)
    return holder


def sum_ring(blocks, axes, dim):
    me = lax.axis_index(axes)
    total = take(blocks, me, dim).astype(f32)
    for distance in (1, 2, 3):
        leaving = take(blocks, (me + distance) % 4, dim)
        total = total + shifted(leaving, axes, distance).astype(f32)
    return total


def sum_plane(first, second):
    first = sum_ring(first, Y_RING, 0).astype(bf16)
    second = sum_ring(second, X_RING, 1).astype(bf16)
    return sum_ring(first, X_RING, 0), sum_ring(second, Y_RING, 0)


def dot(left, right):
    return jnp.dot(left, right, preferred_element_type=f32)


def dot_turned(left, right):
    return lax.dot_general(left, right, (((1,), (1,)), ((), ())), preferred_element_type=f32)


def dot_rows(left, right):
    return lax.dot_general(left, right, (((0,), (0,)), ((), ())), preferred_element_type=f32)


def call(kernel, outs, inputs, scalars, scratch, flops):
    spaces = [pltpu.SMEM] * scalars + [pltpu.VMEM] * (len(inputs) - scalars)
    nbytes = sum(x.size * x.dtype.itemsize for x in list(inputs) + list(outs))
    return pl.pallas_call(
        kernel,
        out_shape=outs,
        in_specs=[pl.BlockSpec(memory_space=space) for space in spaces],
        out_specs=[pl.BlockSpec(memory_space=pltpu.VMEM) for _ in outs],
        scratch_shapes=scratch,
        compiler_params=pltpu.CompilerParams(vmem_limit_bytes=40 << 20),
        cost_estimate=pl.CostEstimate(flops=flops, bytes_accessed=nbytes, transcendentals=0),
    )(*inputs)


def assemble_kernel(rank, few, core, chooser, mine_a, mine_b, other_a, other_b, weights, gram):
    sections, half = weights.shape[0], mine_a.shape[2]
    for s in range(sections):
        for x_hi in range(2):
            for mine, a, b in ((True, mine_a, mine_b), (False, other_a, other_b)):
                owner = core[0] if mine else 1 - core[0]
                for number, source in ((0, a), (1, b)):
                    at = pl.multiple_of((4 * x_hi + number + 2 * owner) * half, half)
                    weights[s, pl.ds(at, half), :] = source[s % 4, 2 * (s // 4) + x_hi]
    left = [dot_turned(chooser[...], weights[s, :, rank:]) for s in range(sections)]
    left = jnp.concatenate(left, axis=0).astype(bf16)
    for t in range(sections):
        found = dot(left, weights[t])
        for s in range(t + 1):
            for kind in (0, 1) if s < t else (1,):
                unit = t * t + 2 * s + (kind if s < t else 0)
                gram[unit // 8, :, (unit % 8) * rank : (unit % 8 + 1) * rank] = found[
                    few * s : few * (s + 1), kind * rank : (kind + 1) * rank
                ]


def products_kernel(rank, hidden, seed, weights, products):
    planes, part, _ = products.shape
    for s in range(weights.shape[0]):
        at = 3 * rank * s
        plain = dot(hidden[...], weights[s])
        turned = dot(seed[...], weights[s, :, rank:])
        for z in range(planes):
            rows = slice(part * z, part * (z + 1))
            products[z, :, at : at + 2 * rank] = plain[rows].astype(bf16)
            products[z, :, at + 2 * rank : at + 3 * rank] = turned[rows].astype(bf16)


def recursion_kernel(
    width, sections, rank, core, products, energy_in, mine_a, mine_b, other_a, other_b, results
):
    half = rank // 2
    part = products.shape[0]
    lowest = jnp.full((part, half), core[0], jnp.int32) == 0

    def unit(number):
        mine, other = (mine_a, other_a) if number < 32 else (mine_b, other_b)
        number = number % 32
        columns = slice((number % 8) * rank, (number % 8 + 1) * rank)
        return mine[number // 8, :, columns], other[number // 8, :, columns]

    def ordered(low, high):
        return jnp.where(lowest, low, high), jnp.where(lowest, high, low)

    def dot_unit(left, number):
        mine, other = unit(number)
        return dot(left[0], mine) + dot(left[1], other)

    energy = energy_in[...]
    activated, before, inverse, outward = [], [], [], []
    for s in range(sections):
        at = 3 * rank * s
        total = products[:, at : at + rank]
        along = products[:, at + rank : at + 2 * rank]
        for t in range(s):
            total = total + dot_unit(activated[t], s * s + 2 * t)
            along = along + dot_unit(activated[t], s * s + 2 * t + 1)
        inverse_s = lax.rsqrt(energy / width + norm_epsilon)
        before_s = total * inverse_s
        activated_s = before_s * jax.nn.sigmoid(before_s)
        rounded = activated_s.astype(bf16).astype(f32)
        results[:, rank * s : rank * (s + 1)] = rounded
        pieces = [x.astype(bf16) for x in ordered(rounded[:, :half], rounded[:, half:])]
        moved = along + dot_unit(pieces, s * s + 2 * s)
        energy = energy + jnp.sum(rounded * (along + moved), axis=-1, keepdims=True)
        activated.append(pieces)
        before.append(before_s)
        inverse.append(inverse_s)
        outward.append(moved)
    pulls, drags = [None] * sections, [None] * sections
    later = jnp.zeros_like(energy)
    lanes = lax.broadcasted_iota(jnp.int32, (part, 128), 1)
    shares = jnp.zeros((part, 128), f32)
    for s in reversed(range(sections)):
        at = 3 * rank * s + 2 * rank
        grad = products[:, at : at + rank] - later * outward[s]
        if s < sections - 1:
            gained, gained_other = jnp.zeros((part, half), f32), jnp.zeros((part, half), f32)
            for t in range(s + 1, sections):
                for left, number in ((pulls[t], t * t + 2 * s), (drags[t], t * t + 2 * s + 1)):
                    mine, other = unit(number)
                    gained = gained + dot_turned(left, mine)
                    gained_other = gained_other + dot_turned(left, other)
            grad = grad + jnp.concatenate(ordered(gained, gained_other), axis=1)
        sigmoid_value = jax.nn.sigmoid(before[s])
        grad_before = grad * sigmoid_value * (1.0 + before[s] * (1.0 - sigmoid_value))
        share = (
            inverse[s] * inverse[s] * jnp.sum(grad_before * before[s], axis=-1, keepdims=True) / width
        )
        pull = inverse[s] * grad_before
        results[:, rank * (sections + s) : rank * (sections + s + 1)] = pull
        pulls[s] = pull.astype(bf16)
        drags[s] = (-later * results[:, rank * s : rank * (s + 1)]).astype(bf16)
        shares = jnp.where(lanes == s, share, shares)
        later = later + share
    results[:, 2 * rank * sections :] = shares


def wide_kernel(rank, grad_scale, hidden, seed, found, weights, uppers, grads, states):
    sections, planes, part, _ = uppers.shape
    half = grads.shape[4]
    tail = found[:, 2 * rank * sections :].astype(f32)
    state = hidden[...].astype(f32)
    states[0] = state
    for s in range(sections - 1):
        state = state + dot_turned(found[:, rank * s : rank * (s + 1)], weights[s, :, rank:])
        states[s + 1] = state
    upstream = seed[...].astype(f32)
    for s in reversed(range(sections)):
        act = found[:, rank * s : rank * (s + 1)]
        pull = found[:, rank * (sections + s) : rank * (sections + s + 1)]
        first = (dot_rows(states[s].astype(bf16), pull) * grad_scale).astype(bf16)
        second = (dot_rows(upstream.astype(bf16), act) * grad_scale).astype(bf16)
        for x_hi in range(2):
            for core in range(2):
                for number in range(2):
                    at = (4 * x_hi + 2 * core + number) * half
                    place = (core, number, s % 4, 2 * (s // 4) + x_hi)
                    grads[place + (slice(None), slice(0, rank))] = first[at : at + half]
                    grads[place + (slice(None), slice(rank, 2 * rank))] = second[at : at + half]
        share = tail[:, s : s + 1] + tail[:, sections + s : sections + s + 1]
        upstream = upstream + dot_turned(pull, weights[s, :, :rank]) - share * states[s]
        for z in range(planes):
            uppers[s, z] = upstream[part * z : part * (z + 1)].astype(bf16)


def body(inputs, cotangent, in_weight, out_weight, norm_gain, lengths):
    micro_count, tok_rows, width = inputs.shape
    feature_rows, rank = in_weight.shape[1:]
    sections, planes = SIZES[0] * SIZES[1], SIZES[2]
    rows = micro_count * tok_rows
    part = rows // sections
    slab = width // planes
    grad_scale = 1.0 / math.sqrt(width_rows(micro_count, tok_rows))
    section = lax.axis_index(SECTION)
    replica = lax.axis_index(REP)

    gain = lax.dynamic_slice(norm_gain[0], (replica * feature_rows,), (feature_rows,))
    scaled_in = (in_weight[0].astype(f32) * gain[:, None]).astype(bf16)
    own = jnp.concatenate((scaled_in, out_weight[0]), axis=1)
    half = feature_rows // 2
    started = [gather_ring(own[:half], X_RING, 0), gather_ring(own[half:], Y_RING, 0)]

    own_hidden = lax.dynamic_slice(inputs.reshape(rows, width), (part * section, 0), (part, width))
    own_seed = lax.dynamic_slice(cotangent.reshape(rows, width), (part * section, 0), (part, width))
    numbers = part * section + jnp.arange(part, dtype=jnp.int32)
    micro, place = numbers // tok_rows, numbers % tok_rows
    limit = jnp.sum(
        jnp.where(micro[:, None] == jnp.arange(micro_count)[None, :], lengths, 0), axis=1
    )
    own_seed = jnp.where((place < limit)[:, None], own_seed, jnp.zeros((), bf16))
    energy = jnp.sum(jnp.square(own_hidden.astype(f32)), axis=-1, keepdims=True)
    pair = jnp.stack((own_hidden, own_seed), axis=0).reshape(2, part, planes, slab)
    started, pair = lax.optimization_barrier((started, jnp.transpose(pair, (2, 0, 1, 3))))
    halves = [gather_ring(started[0], Y_RING, 0), gather_ring(started[1], X_RING, 1)]
    pair = exchange(pair, ("z",))
    halves, pair, energy = lax.optimization_barrier((halves, pair, energy))
    others = [swap_core(x) for x in halves]
    hidden = pair[:, 0].reshape(rows, slab)
    seed = pair[:, 1].reshape(rows, slab)

    x_place, y_place = lax.axis_index(X_RING), lax.axis_index(Y_RING)
    strip = (lax.axis_index("core") * 4 + y_place) * 4 + x_place
    few = rank // 32
    picked = strip * few + jnp.arange(few, dtype=jnp.int32)
    chooser = (picked[:, None] == jnp.arange(rank)[None, :]).astype(bf16)
    core = lax.axis_index("core").astype(jnp.int32)[None]
    weights, gram = call(
        functools.partial(assemble_kernel, rank, few),
        (
            jax.ShapeDtypeStruct((sections, slab, 2 * rank), bf16),
            jax.ShapeDtypeStruct((planes, few, sections * rank), f32),
        ),
        (core, chooser, *halves, *others),
        1,
        [],
        2 * sections * sections * few * slab * 2 * rank,
    )
    gram = exchange(gram.astype(bf16), ("z",))
    gram = jnp.sum(gram.astype(f32), axis=0).astype(bf16)
    gram = spread(gram, ("z",))
    grams = gather_plane(gram[: planes // 2], gram[planes // 2 :], 1)
    grams = [x.reshape(planes // 2, rank // 2, -1) for x in grams]
    other_grams = [swap_core(x) for x in grams]

    (products,) = call(
        functools.partial(products_kernel, rank),
        (jax.ShapeDtypeStruct((planes, part, 3 * rank * sections), bf16),),
        (hidden, seed, weights),
        0,
        [],
        2 * rows * slab * 3 * rank * sections,
    )
    products = jnp.sum(exchange(products, ("z",)).astype(f32), axis=0)

    (found,) = call(
        functools.partial(recursion_kernel, width, sections, rank),
        (jax.ShapeDtypeStruct((part, 2 * rank * sections + 128), f32),),
        (core, products, energy, *grams, *other_grams),
        1,
        [],
        2 * part * rank * rank * 120,
    )
    shares = found[:, 2 * rank * sections : 2 * rank * sections + sections]
    shares_high = shares.astype(bf16)
    shares_low = (shares - shares_high.astype(f32)).astype(bf16)
    filler = jnp.zeros((part, 128 - 2 * sections), bf16)
    found = jnp.concatenate(
        [found[:, : 2 * rank * sections].astype(bf16), shares_high, shares_low, filler], axis=1
    )
    found = gather_z(found).reshape(rows, -1)

    uppers, grads = call(
        functools.partial(wide_kernel, rank, grad_scale),
        (
            jax.ShapeDtypeStruct((sections, planes, part, slab), bf16),
            jax.ShapeDtypeStruct((2, 2, 4, 4, half, 2 * rank), bf16),
        ),
        (hidden, seed, found, weights),
        0,
        [pltpu.VMEM((sections, rows, slab), f32)],
        8 * rows * slab * rank * sections,
    )
    uppers = exchange(uppers.reshape(sections * planes, part, slab), SECTION + ("z",))

    me = lax.axis_index("core")
    other = swap_core(take(grads, 1 - me, 0))
    grads = (take(grads, me, 0).astype(f32) + other.astype(f32)).astype(bf16)
    grads = jnp.concatenate(sum_plane(grads[0], grads[1]), axis=0)
    grads, uppers = lax.optimization_barrier((grads, uppers))
    uppers = uppers.reshape(sections, planes, part, slab)
    grad_inputs = jnp.transpose(uppers, (0, 2, 1, 3)).reshape(1, micro_count, tok_rows, width)
    raw_in = grads[:, :rank]
    grad_in_weight = (raw_in * gain[:, None]).astype(bf16)[None]
    grad_out_weight = grads[:, rank:].astype(bf16)[None]
    gain_part = jnp.sum(raw_in * in_weight[0].astype(f32), axis=1)
    grad_gain = spread(gain_part, REP).reshape(1, width)
    return (grad_in_weight, grad_out_weight, grad_gain, grad_inputs)


def width_rows(micro_count, tok_rows):
    return micro_count * tok_rows * SIZES[2] * SIZES[3] * SIZES[4]


def solution(mesh):
    fine = Mesh(np.asarray(mesh.devices).reshape(SIZES), AXES)
    in_specs = (
        P(None, REP, None),
        P(None, REP, None),
        P(SECTION, REP, None),
        P(SECTION, REP, None),
        P(SECTION, None),
        P(REP, None),
    )
    out_specs = (
        P(SECTION, REP, None),
        P(SECTION, REP, None),
        P(SECTION, None),
        P(SECTION, None, REP, None),
    )
    return jax.shard_map(body, mesh=fine, in_specs=in_specs, out_specs=out_specs, check_vma=False)
```
